768 devices in a mesh: dp: 32 (over z_hi, y, core), tensor: 24 (over z_lo, x).
Axes of the slice: x: 4, y: 8, z: 12 (z_hi: 2, z_lo: 6; z = z_hi * 6 + z_lo), core: 2. Of those that a mesh axis runs over, the one named last changes fastest.
Arguments:
- attention: bfloat16 [6144, 6144], P('dp', 'tensor'), may hold values from -6 to 6
- out_proj: bfloat16 [6144, 8192], P('tensor'), may hold values from -0.078125 to 0.078125
- residual: bfloat16 [6144, 8192], P(('dp', 'tensor')), may hold values from -6 to 6
- gain: float32 [8192], replicated, may hold values from 0.1 to 1.9
- grad_normed: bfloat16 [6144, 8192], P(('dp', 'tensor')), may hold values from -6 to 6
- grad_residual: bfloat16 [6144, 8192], P(('dp', 'tensor')), may hold values from -6 to 6
Outputs:
- normed: bfloat16 [6144, 8192], P(('dp', 'tensor'))
- grad_mixed: bfloat16 [6144, 8192], P(('dp', 'tensor'))
- grad_attention: bfloat16 [6144, 6144], P('dp', 'tensor')
- grad_out_proj: float32 [6144, 8192], P('tensor', 'dp')
The draws below stay inside these ranges and needn't reach their ends.
All inputs are finite; a program needn't handle non-finite values.
Results may differ from the reference program's by a relative error of at most 0.02.
Values may be sent and summed in bfloat16 or wider, within the bound.
No kernel may reach another device: no remote copies, remote signals or barrier semaphores. Data moves between devices by JAX's collectives and lax.ppermute only.
A program may use at most 32 MiB of HBM per device.

```python
import jax
import jax.numpy as jnp
from jax import lax

D = 8192
HEAD_DIM = 128
HEADS_DEV = 2
TOK_DEV = 192
HEADS = 48
TOKENS = 6144
N_DP = 32
N_TENSOR = 24


def levels(stream_key, dims, split, low, top_value):
    level, own = 1.0, jax.random.fold_in(stream_key, 6)
    for axis_at, parts in split:
        steps = jnp.exp(jax.random.uniform(jax.random.fold_in(own, axis_at), (parts,), jnp.float32, low / len(split), top_value / len(split)))
        level = level * jnp.repeat(steps, dims[axis_at] // parts).reshape([-1 if axis == axis_at else 1 for axis in range(len(dims))])
    return level


def centred(stream_key, dims, deviation, most, cuts=(), kind=jnp.bfloat16):
    level = levels(stream_key, dims, cuts, -0.22, 0.18) if cuts else 1.0
    result = jax.random.normal(stream_key, dims, jnp.float32) * deviation * level
    return jnp.minimum(jnp.maximum(result, -most), most).astype(kind)


def setup_inputs(seed: int = 0) -> dict:
    streams_of = jax.random.split(jax.random.key(seed), 7)
    return {
        "attention": centred(streams_of[0], (TOKENS, HEADS * HEAD_DIM), 1.0, 6.0, ((0, 32), (1, 24))),
        "out_proj": centred(streams_of[1], (HEADS * HEAD_DIM, D), (HEADS * HEAD_DIM) ** -0.5, 0.078125, ((0, 24),)),
        "residual": centred(streams_of[2], (TOKENS, D), 1.0, 6.0, ((0, 768),)),
        "gain": jnp.clip(1.0 + 0.18 * jax.random.normal(streams_of[3], (D,), jnp.float32), 0.1, 1.9),
        "grad_normed": centred(streams_of[4], (TOKENS, D), 1.0, 6.0, ((0, 768),)),
        "grad_residual": centred(streams_of[5], (TOKENS, D), 1.0, 6.0, ((0, 768),)),
    }


def reference(attention, out_proj, residual, gain, grad_normed, grad_residual):
    width = HEADS_DEV * HEAD_DIM
    grouped_heads = attention.reshape(TOKENS, N_TENSOR, width).transpose(1, 0, 2)
    grouped_weight = out_proj.reshape(N_TENSOR, width, D)

    def add_group(running, pieces):
        part = jnp.dot(pieces[0], pieces[1], preferred_element_type=jnp.float32).astype(jnp.bfloat16)
        return (running + part.astype(jnp.float32), None)
    mixed, _ = lax.scan(add_group, residual.astype(jnp.float32), (grouped_heads, grouped_weight))
    rms = jnp.sqrt(lax.optimization_barrier(jnp.mean(mixed * mixed, axis=-1, keepdims=True)) + 1e-05)
    unit = mixed / rms
    normed = (unit * gain).astype(jnp.bfloat16)
    scaled = grad_normed.astype(jnp.float32) * gain
    inner = lax.optimization_barrier(jnp.mean(scaled * unit, axis=-1, keepdims=True))
    grad_mixed = (grad_residual.astype(jnp.float32) + (scaled - unit * inner) / rms).astype(jnp.bfloat16)
    grad_attention = jnp.dot(grad_mixed, out_proj.T, preferred_element_type=jnp.float32).astype(jnp.bfloat16)
    token_blocks = attention.reshape(N_DP, TOK_DEV, HEADS * HEAD_DIM)
    grad_blocks = grad_mixed.reshape(N_DP, TOK_DEV, D)

    def add_block(running, pieces):
        term = jnp.dot(pieces[0].T, pieces[1], preferred_element_type=jnp.float32).astype(jnp.bfloat16)
        return (running + term.astype(jnp.float32), None)
    start = jnp.zeros((HEADS * HEAD_DIM, D), jnp.float32)
    grad_out_proj, _ = lax.scan(add_block, start, (token_blocks, grad_blocks))
    return (normed, grad_mixed, grad_attention, grad_out_proj)
```

```python
import jax
import jax.numpy as jnp
from jax import lax
from jax.experimental import pallas as pl
from jax.experimental.pallas import tpu as pltpu
from jax.sharding import Mesh, PartitionSpec as P

ZH, Y, CORE, ZL, X = 2, 8, 2, 6, 4
BF, F32 = jnp.bfloat16, jnp.float32
D = 8192
CHUNKS = 2
VMEM = 48 * 1024 * 1024


def shift(value, axis, size, move):
    return lax.ppermute(value, axis, [(i, move(i)) for i in range(size)])


def to_x(value, r):
    return shift(value, "x", X, lambda i: (i - r) % X)


def to_q(value):
    return shift(value, "zl", ZL, lambda i: i ^ 1)


def to_p(value, r):
    return shift(value, "zl", ZL, lambda i: ((i // 2 - r) % 3) * 2 + i % 2)


def to_v(value):
    return shift(value, "y", Y, lambda i: i ^ 1)


def to_u(value, r):
    return shift(value, "y", Y, lambda i: ((i // 2 - r) % 4) * 2 + i % 2)


def to_core(value):
    return shift(value, "core", CORE, lambda i: i ^ 1)


def to_zh(value):
    return shift(value, "zh", ZH, lambda i: i ^ 1)


def norm_kernel(place, *refs):
    sums = refs[: 3 * CHUNKS]
    residual, gain, grad_normed, grad_residual, normed, grad_mixed, mine, other = refs[3 * CHUNKS :]
    share = jnp.concatenate(
        [
            sums[3 * c][...] + sums[3 * c + 1][...].astype(F32) + sums[3 * c + 2][...].astype(F32)
            for c in range(CHUNKS)
        ],
        axis=1,
    )
    mixed = residual[...].astype(F32) + share
    rms = jnp.sqrt(jnp.mean(mixed * mixed, axis=-1, keepdims=True) + 1e-05)
    unit = mixed / rms
    normed[...] = (unit * gain[...]).astype(BF)
    scaled = grad_normed[...].astype(F32) * gain[...]
    inner = jnp.mean(scaled * unit, axis=-1, keepdims=True)
    grad_mixed[...] = (grad_residual[...].astype(F32) + (scaled - unit * inner) / rms).astype(BF)
    core, zh = place[0], place[1]
    for k in range(2):
        half = (1 - zh) if k == 0 else zh
        for y in range(Y):
            at = (half * Y + y) * 2
            put = pl.ds(k * 2048 + y * 256, 256)
            mine[:, put] = grad_mixed[:, pl.ds(pl.multiple_of((at + core) * 256, 256), 256)]
            other[:, put] = grad_mixed[:, pl.ds(pl.multiple_of((at + 1 - core) * 256, 256), 256)]


def norm(place, sums, residual, gain, grad_normed, grad_residual):
    whole = pl.BlockSpec(memory_space=pltpu.VMEM)
    count = len(sums) + 4
    return pl.pallas_call(
        norm_kernel,
        out_shape=(
            jax.ShapeDtypeStruct((8, D), BF),
            jax.ShapeDtypeStruct((8, D), BF),
            jax.ShapeDtypeStruct((8, D // 2), BF),
            jax.ShapeDtypeStruct((8, D // 2), BF),
        ),
        in_specs=[pl.BlockSpec(memory_space=pltpu.SMEM)] + [whole] * count,
        out_specs=(whole,) * 4,
        compiler_params=pltpu.CompilerParams(vmem_limit_bytes=16 * 1024 * 1024),
        cost_estimate=pl.CostEstimate(flops=8 * D * 20, bytes_accessed=8 * D * 20, transcendentals=0),
        name="norm",
    )(place, *sums, residual, gain, grad_normed, grad_residual)


def term_kernel(blocks, turned, *refs):
    pieces, send, keep = refs[:X], refs[X], refs[X + 1]
    for r in range(Y):
        at = pl.ds(pl.multiple_of(blocks[r] * 256, 256), 256)
        total = jnp.zeros((256, 256), F32)
        for x in range(X):
            total += jnp.dot(
                turned[:, x * 96 : (x + 1) * 96], pieces[x][:, at], preferred_element_type=F32
            )
        out = keep if r < 4 else send
        out[(r % 4) * 256 : (r % 4 + 1) * 256, :] = total.astype(BF)


def term_parts(blocks, turned, pieces):
    whole = pl.BlockSpec(memory_space=pltpu.VMEM)
    return pl.pallas_call(
        term_kernel,
        out_shape=(jax.ShapeDtypeStruct((1024, 256), BF),) * 2,
        in_specs=[pl.BlockSpec(memory_space=pltpu.SMEM)] + [whole] * 5,
        out_specs=(whole,) * 2,
        compiler_params=pltpu.CompilerParams(vmem_limit_bytes=VMEM),
        cost_estimate=pl.CostEstimate(
            flops=2 * 256 * 384 * 2048, bytes_accessed=3 * 1024 * 1024, transcendentals=0
        ),
        name="term",
    )(blocks, turned, *pieces)


def back_kernel(at, *refs):
    pieces, weight, out = refs[:X], refs[X], refs[X + 1]

    @pl.when(pl.program_id(0) == 0)
    def _():
        out[...] = jnp.zeros_like(out)

    for x in range(X):
        out[x * 96 : (x + 1) * 96, :] += lax.dot_general(
            pieces[x][...], weight[...], (((1,), (1,)), ((), ())), preferred_element_type=F32
        )


def back(first, pieces, weight):
    return pl.pallas_call(
        back_kernel,
        out_shape=jax.ShapeDtypeStruct((384, 256), F32),
        grid_spec=pltpu.PrefetchScalarGridSpec(
            num_scalar_prefetch=1,
            grid=(Y,),
            in_specs=[pl.BlockSpec((96, 256), lambda y, at: (0, y))] * X
            + [pl.BlockSpec((256, 256), lambda y, at: (0, at[0] + 2 * y))],
            out_specs=pl.BlockSpec((384, 256), lambda y, at: (0, 0)),
        ),
        compiler_params=pltpu.CompilerParams(vmem_limit_bytes=16 * 1024 * 1024),
        cost_estimate=pl.CostEstimate(
            flops=2 * 256 * 384 * 2048, bytes_accessed=3 * 1024 * 1024, transcendentals=0
        ),
        name="back",
    )(first, *pieces, weight)


def per_device(attention, out_proj, residual, gain, grad_normed, grad_residual):
    x, zl, y = lax.axis_index("x"), lax.axis_index("zl"), lax.axis_index("y")
    core, zh = lax.axis_index("core"), lax.axis_index("zh")

    r = jnp.arange(24, dtype=jnp.int32)
    owner_x = (x - r // 6 + X) % X
    owner_q = (zl % 2) ^ ((r // 3) % 2)
    owner_p = (zl // 2 - r % 3 + 3) % 3
    owner = (owner_p * 2 + owner_q) * X + owner_x
    token = jnp.repeat(owner * 8, 8) + jnp.tile(jnp.arange(8, dtype=jnp.int32), 24)
    order = (token[:, None] == jnp.arange(192, dtype=jnp.int32)[None, :]).astype(BF)
    near = jnp.dot(order, attention, preferred_element_type=F32).astype(BF)

    width = D // CHUNKS
    sums = []
    for c in range(CHUNKS):
        weight = out_proj[:, c * width : (c + 1) * width]

        def product(r):
            return jnp.dot(near[r * 48 : (r + 1) * 48], weight, preferred_element_type=F32)

        got = [to_x(product(r).astype(BF), r) for r in (2, 1, 3)]
        summed = product(0) + got[0].astype(F32) + got[1].astype(F32) + got[2].astype(F32)
        pair = to_q(summed[24:].astype(BF))
        summed = summed[:24] + pair.astype(F32)
        sums += [summed[:8]] + [to_p(summed[r * 8 : (r + 1) * 8].astype(BF), r) for r in (1, 2)]

    far = to_core(near)
    both = jnp.stack([near.reshape(24, 8, 256), far.reshape(24, 8, 256)], axis=1).reshape(384, 256)
    turned = both.T

    place = jnp.stack([core, zh]).astype(jnp.int32)
    normed, grad_mixed, mine, other = norm(
        place, sums, residual, gain.reshape(1, D), grad_normed, grad_residual
    )
    other = to_core(other)
    s = jnp.arange(Y, dtype=jnp.int32)
    blocks = ((y // 2 - s % 4 + 4) % 4) * 2 + ((y % 2) ^ (s // 4))

    grads, terms = 0.0, []
    for k in range(2):
        half = (1 - zh) if k == 0 else zh
        at = slice(k * 2048, (k + 1) * 2048)
        own = jnp.concatenate([mine[:, at], other[:, at]], axis=0)
        line = jnp.concatenate([own, to_p(own, -1), to_p(own, -2)], axis=0)
        line = jnp.concatenate([line, to_q(line)], axis=0)
        pieces = [line] + [to_x(line, -r) for r in (1, 2, 3)]
        send, keep = term_parts(blocks, turned, pieces)
        kept = keep.astype(F32) + to_v(send).astype(F32)
        total = kept[:256]
        for r in (1, 2, 3):
            total = total + to_u(kept[r * 256 : (r + 1) * 256].astype(BF), r).astype(F32)
        terms.append(total)
        first = (half * 16 + core).reshape(1).astype(jnp.int32)
        grads = grads + back(first, pieces, out_proj)
    grad_out_proj = terms[1] + to_zh(terms[0].astype(BF)).astype(F32)

    grads = grads.reshape(24, 2, 8, 256)
    ours = grads[:, 0].reshape(192, 256) + to_core(grads[:, 1].reshape(192, 256))
    grad_attention = lax.dot_general(
        order, ours.astype(BF), (((0,), (0,)), ((), ())), preferred_element_type=F32
    ).astype(BF)
    return (normed, grad_mixed, grad_attention, grad_out_proj)


def solution(mesh):
    dp, tensor = ("zh", "y", "core"), ("zl", "x")
    fine = Mesh(mesh.devices.reshape(ZH, Y, CORE, ZL, X), dp + tensor)
    rows = P(dp + tensor, None)
    return jax.shard_map(
        per_device,
        mesh=fine,
        in_specs=(P(dp, tensor), P(tensor, None), rows, P(), rows, rows),
        out_specs=(rows, rows, P(dp, tensor), P(tensor, dp)),
        check_vma=False,
    )
```

```python
import functools

import jax
import jax.numpy as jnp
from jax import lax
from jax.experimental import pallas as pl
from jax.experimental.pallas import tpu as pltpu
from jax.sharding import Mesh, PartitionSpec as P

ZH, Y, CORE, ZL, X = 2, 8, 2, 6, 4
BF, F32 = jnp.bfloat16, jnp.float32
D = 8192
PIECES = 10
VMEM = 24 * 1024 * 1024


def shift(value, axis, size, move):
    return lax.ppermute(value, axis, [(i, move(i)) for i in range(size)])


def to_x(value, r):
    return shift(value, "x", X, lambda i: (i - r) % X)


def to_q(value):
    return shift(value, "zl", ZL, lambda i: i ^ 1)


def to_p(value, r):
    return shift(value, "zl", ZL, lambda i: ((i // 2 - r) % 3) * 2 + i % 2)


def to_v(value):
    return shift(value, "y", Y, lambda i: i ^ 1)


def to_u(value, r):
    return shift(value, "y", Y, lambda i: ((i // 2 - r) % 4) * 2 + i % 2)


def to_core(value):
    return shift(value, "core", CORE, lambda i: i ^ 1)


def to_zh(value):
    return shift(value, "zh", ZH, lambda i: i ^ 1)


def product_kernel(near, weight, *refs):
    outs, held, sems = refs[:8], refs[8], refs[9]
    copies = [
        pltpu.make_async_copy(
            weight.at[:, c * 1024 : (c + 1) * 1024], held.at[:, c * 1024 : (c + 1) * 1024], sems.at[c]
        )
        for c in range(8)
    ]
    for copy in copies:
        copy.start()
    for c in range(8):
        copies[c].wait()
        at = slice(c * 1024, (c + 1) * 1024)
        total = jnp.dot(near[...], held[:, at], preferred_element_type=F32)
        for r in range(8):
            outs[r][:, at] = total[r * 24 : (r + 1) * 24].astype(BF)


def products(near, weight):
    whole = pl.BlockSpec(memory_space=pltpu.VMEM)
    return pl.pallas_call(
        product_kernel,
        out_shape=(jax.ShapeDtypeStruct((24, D), BF),) * 8,
        in_specs=[whole, pl.BlockSpec(memory_space=pltpu.HBM)],
        out_specs=(whole,) * 8,
        scratch_shapes=[pltpu.VMEM((256, D), BF), pltpu.SemaphoreType.DMA((8,))],
        compiler_params=pltpu.CompilerParams(vmem_limit_bytes=VMEM),
        cost_estimate=pl.CostEstimate(
            flops=2 * 192 * 256 * D, bytes_accessed=(256 + 192) * 2 * D, transcendentals=0
        ),
        name="products",
    )(near, weight)


def forward_kernel(value, arrived, held, near, out, held_out, near_out):
    out[...] = (value[...].astype(F32) + arrived[...].astype(F32)).astype(BF)
    held_out[...] = held[...]
    near_out[...] = near[...]


def forward(value, arrived, held, near):
    block = pl.BlockSpec((24, 4096), lambda c: (0, c))
    rows = pl.BlockSpec((192, 128), lambda c: (0, c))
    return pl.pallas_call(
        forward_kernel,
        out_shape=(jax.ShapeDtypeStruct((24, D), BF),) * 2 + (jax.ShapeDtypeStruct((192, 256), BF),),
        grid=(2,),
        in_specs=[block] * 3 + [rows],
        out_specs=(block, block, rows),
        compiler_params=pltpu.CompilerParams(vmem_limit_bytes=16 * 1024 * 1024),
        cost_estimate=pl.CostEstimate(flops=24 * D, bytes_accessed=24 * D * 10, transcendentals=0),
        name="forward",
    )(value, arrived, held, near)


def after_q_kernel(keep, left, right, pair, own, one, two):
    total = keep[...].astype(F32) + left[...].astype(F32)
    total = total + right[...].astype(F32) + pair[...].astype(F32)
    own[...] = total[:8]
    one[...] = total[8:16].astype(BF)
    two[...] = total[16:].astype(BF)


def after_q(keep, left, right, pair):
    block = pl.BlockSpec((24, 2048), lambda c: (0, c))
    rows = pl.BlockSpec((8, 2048), lambda c: (0, c))
    return pl.pallas_call(
        after_q_kernel,
        out_shape=tuple(jax.ShapeDtypeStruct((8, D), kind) for kind in (F32, BF, BF)),
        grid=(D // 2048,),
        in_specs=[block] * 4,
        out_specs=(rows,) * 3,
        compiler_params=pltpu.CompilerParams(vmem_limit_bytes=16 * 1024 * 1024),
        cost_estimate=pl.CostEstimate(flops=24 * D * 4, bytes_accessed=24 * D * 10, transcendentals=0),
        name="after_q",
    )(keep, left, right, pair)


def norm_kernel(place, first, second, third, *refs):
    residual, gain, grad_normed, grad_residual, late, normed, grad_mixed, mine, other = refs
    share = first[...] + second[...].astype(F32) + third[...].astype(F32)
    mixed = residual[...].astype(F32) + share
    rms = jnp.sqrt(jnp.mean(mixed * mixed, axis=-1, keepdims=True) + 1e-05)
    unit = mixed / rms
    normed[...] = (unit * gain[...]).astype(BF)
    scaled = grad_normed[...].astype(F32) * gain[...]
    inner = jnp.mean(scaled * unit, axis=-1, keepdims=True)
    grad_mixed[...] = (grad_residual[...].astype(F32) + (scaled - unit * inner) / rms).astype(BF)
    core, zh, v = place[0], place[1], place[2]
    for side in range(2):
        for k in range(2):
            for u in range(4):
                half = (1 - zh) if k == 0 else zh
                at = (half * Y + u * 2 + (v if side == 0 else 1 - v)) * 2
                put = pl.ds(side * 2048 + k * 1024 + u * 256, 256)
                mine[:, put] = grad_mixed[:, pl.ds(pl.multiple_of((at + core) * 256, 256), 256)]
                other[:, put] = grad_mixed[:, pl.ds(pl.multiple_of((at + 1 - core) * 256, 256), 256)]


def norm(place, sums, residual, gain, grad_normed, grad_residual, late):
    whole = pl.BlockSpec(memory_space=pltpu.VMEM)
    count = len(sums) + 4
    return pl.pallas_call(
        norm_kernel,
        out_shape=(
            jax.ShapeDtypeStruct((8, D), BF),
            jax.ShapeDtypeStruct((8, D), BF),
            jax.ShapeDtypeStruct((8, D // 2), BF),
            jax.ShapeDtypeStruct((8, D // 2), BF),
        ),
        in_specs=[pl.BlockSpec(memory_space=pltpu.SMEM)]
        + [whole] * count
        + [pl.BlockSpec(memory_space=pl.ANY)],
        out_specs=(whole,) * 4,
        compiler_params=pltpu.CompilerParams(vmem_limit_bytes=16 * 1024 * 1024),
        cost_estimate=pl.CostEstimate(flops=8 * D * 20, bytes_accessed=8 * D * 20, transcendentals=0),
        name="norm",
    )(place, *sums, residual, gain, grad_normed, grad_residual, late)


def term_kernel(blocks, turned, *refs):
    pieces, outs = refs[:PIECES], refs[PIECES + 1 :]
    for k in range(2):
        for r in range(4):
            at = pl.ds(pl.multiple_of((k * 4 + blocks[r]) * 256, 256), 256)
            block = jnp.concatenate([piece[:, at] for piece in pieces], axis=0)
            total = jnp.dot(turned[...], block, preferred_element_type=F32)
            outs[k * 4 + r][...] = total.astype(outs[k * 4 + r].dtype)


def term_parts(blocks, turned, pieces, late):
    whole = pl.BlockSpec(memory_space=pltpu.VMEM)
    return pl.pallas_call(
        term_kernel,
        out_shape=tuple(jax.ShapeDtypeStruct((256, 256), kind) for kind in (F32, BF, BF, BF) * 2),
        grid=(1,),
        in_specs=[pl.BlockSpec(memory_space=pltpu.SMEM)]
        + [whole] * (1 + PIECES)
        + [pl.BlockSpec(memory_space=pl.ANY)],
        out_specs=(pl.BlockSpec((256, 256), lambda i: (0, 0)),) * 8,
        compiler_params=pltpu.CompilerParams(vmem_limit_bytes=VMEM),
        cost_estimate=pl.CostEstimate(
            flops=2 * 256 * 768 * 2048, bytes_accessed=5 * 1024 * 1024, transcendentals=0
        ),
        name="term",
    )(blocks, turned, *pieces, late)


def back_kernel(count, first, *refs):
    pieces, weight = refs[:count], refs[count]
    out, held, sems = refs[-3:]
    copies = []
    for c in range(8):
        at = pl.ds(pl.multiple_of((first[c // 4] + 4 * (c % 4)) * 256, 256), 256)
        copies.append(pltpu.make_async_copy(weight.at[:, at], held.at[c], sems.at[c]))
        copies[c].start()
    total = jnp.zeros(out.shape, F32)
    for c in range(8):
        copies[c].wait()
        block = jnp.concatenate([piece[:, c * 256 : (c + 1) * 256] for piece in pieces], axis=0)
        total += lax.dot_general(
            block, held[c], (((1,), (1,)), ((), ())), preferred_element_type=F32
        )
    out[...] = total


def back(first, pieces, weight, late):
    whole = pl.BlockSpec(memory_space=pltpu.VMEM)
    rows = sum(piece.shape[0] for piece in pieces)
    return pl.pallas_call(
        functools.partial(back_kernel, len(pieces)),
        out_shape=jax.ShapeDtypeStruct((rows, 256), F32),
        in_specs=[pl.BlockSpec(memory_space=pltpu.SMEM)]
        + [whole] * len(pieces)
        + [pl.BlockSpec(memory_space=pltpu.HBM), pl.BlockSpec(memory_space=pl.ANY)],
        out_specs=whole,
        scratch_shapes=[pltpu.VMEM((8, 256, 256), BF), pltpu.SemaphoreType.DMA((8,))],
        compiler_params=pltpu.CompilerParams(vmem_limit_bytes=VMEM),
        cost_estimate=pl.CostEstimate(
            flops=2 * 256 * rows * 2048, bytes_accessed=3 * 1024 * 1024, transcendentals=0
        ),
        name="back",
    )(first, *pieces, weight, late)


def apart_kernel(*refs):
    pieces, stay, go = refs[:-2], refs[-2], refs[-1]
    place = 0
    for piece in pieces:
        for r in range(piece.shape[0] // 32):
            for k in range(4):
                put = (k // 2) * 192 + place * 8
                out = (stay, go)[k % 2]
                out[put : put + 8, :] = piece[r * 32 + k * 8 : r * 32 + k * 8 + 8, :]
            place += 1


def apart(pieces):
    whole = pl.BlockSpec(memory_space=pltpu.VMEM)
    return pl.pallas_call(
        apart_kernel,
        out_shape=(jax.ShapeDtypeStruct((384, 256), F32),) * 2,
        in_specs=[whole] * len(pieces),
        out_specs=(whole,) * 2,
        compiler_params=pltpu.CompilerParams(vmem_limit_bytes=VMEM),
        cost_estimate=pl.CostEstimate(flops=0, bytes_accessed=1536 * 1024, transcendentals=0),
        name="apart",
    )(*pieces)


def per_device(attention, out_proj, residual, gain, grad_normed, grad_residual):
    x, zl, y = lax.axis_index("x"), lax.axis_index("zl"), lax.axis_index("y")
    core, zh = lax.axis_index("core"), lax.axis_index("zh")

    r = jnp.arange(24, dtype=jnp.int32)
    owner_x = (x - r // 6 + X) % X
    owner_q = (zl % 2) ^ ((r // 3) % 2)
    owner_p = (zl // 2 - r % 3 + 3) % 3
    owner = (owner_p * 2 + owner_q) * X + owner_x
    token = jnp.repeat(owner * 8, 8) + jnp.tile(jnp.arange(8, dtype=jnp.int32), 24)
    order = (token[:, None] == jnp.arange(192, dtype=jnp.int32)[None, :]).astype(BF)
    near = jnp.dot(order, attention, preferred_element_type=F32).astype(BF)

    keep, send, one_keep, one_send, left, right, three_keep, three_send = products(near, out_proj)
    left, right = to_x(left, 1), to_x(right, 3)
    right = to_x((three_send.astype(F32) + right.astype(F32)).astype(BF), 3)
    from_right = to_x(one_send, 1)
    left, three_keep, near_late = forward(one_keep, left, three_keep, near)
    left, from_left = to_x(left, 1), to_x(three_keep, 3)
    send = send.astype(F32) + from_right.astype(F32) + right.astype(F32)
    pair = to_q(send.astype(BF))

    far = to_core(near_late)
    both = jnp.concatenate([near.reshape(24, 8, 256), far.reshape(24, 8, 256)], axis=1)
    both = jnp.concatenate([both, to_v(both)], axis=1)
    turned = both.reshape(768, 256).T
    mine, one, two = after_q(keep, left, from_left, pair)
    sums = (mine, to_p(one, 1), to_p(two, 2))

    u, v = y // 2, y % 2
    place = jnp.stack([core, zh, v]).astype(jnp.int32)
    normed, grad_mixed, mine, other = norm(
        place, sums, residual, gain.reshape(1, D), grad_normed, grad_residual, turned
    )
    other = to_core(other)
    blocks = (u - jnp.arange(4, dtype=jnp.int32) + 4) % 4

    own = jnp.concatenate([mine, other], axis=0)
    own = jnp.concatenate([own[:, :2048], to_v(own[:, 2048:])], axis=0)
    line = jnp.concatenate([own, to_p(own, -1), to_p(own, -2)], axis=0)
    lines = (line, to_q(line))
    ones = [to_x(part, -1) for part in lines]
    threes = [to_x(part, -3) for part in lines]
    twos = [(to_x(one[:48], -1), to_x(three[48:], -3)) for one, three in zip(ones, threes)]
    pieces = [*lines, *ones, *twos[0], *twos[1], *threes]

    first = jnp.stack([1 - zh, zh]).astype(jnp.int32) * 16 + (v * 2 + core).astype(jnp.int32)
    early = back(first, [*lines, *ones, *threes], out_proj, blocks)
    parts = term_parts(blocks, turned, pieces, early)
    got = [[to_u(parts[k * 4 + r], r) for r in (1, 2, 3)] for k in range(2)]
    sums = [parts[k * 4] + sum(value.astype(F32) for value in got[k]) for k in range(2)]
    passing = sums[0].astype(BF)
    grad_out_proj = sums[1] + to_zh(passing).astype(F32)

    late = back(first, [*twos[0], *twos[1]], out_proj, parts[4])
    stay, go = apart([early[:384], late, early[384:]])
    stay = stay + to_core(go)
    ours = stay[:192] + to_v(stay[192:])
    grad_attention = lax.dot_general(
        order, ours.astype(BF), (((0,), (0,)), ((), ())), preferred_element_type=F32
    ).astype(BF)
    return (normed, grad_mixed, grad_attention, grad_out_proj)


def solution(mesh):
    dp, tensor = ("zh", "y", "core"), ("zl", "x")
    fine = Mesh(mesh.devices.reshape(ZH, Y, CORE, ZL, X), dp + tensor)
    rows = P(dp + tensor, None)
    return jax.shard_map(
        per_device,
        mesh=fine,
        in_specs=(P(dp, tensor), P(tensor, None), rows, P(), rows, rows),
        out_specs=(rows, rows, P(dp, tensor), P(tensor, dp)),
        check_vma=False,
    )
```

```python
import functools

import jax
import jax.numpy as jnp
from jax import lax
from jax.experimental import pallas as pl
from jax.experimental.pallas import tpu as pltpu
from jax.sharding import Mesh, PartitionSpec as P

ZH, Y, CORE, ZL, X = 2, 8, 2, 6, 4
BF, F32 = jnp.bfloat16, jnp.float32
D = 8192
PIECES = 8
VMEM = 24 * 1024 * 1024


def shift(value, axis, size, move):
    return lax.ppermute(value, axis, [(i, move(i)) for i in range(size)])


def to_x(value, r):
    return shift(value, "x", X, lambda i: (i - r) % X)


def to_q(value):
    return shift(value, "zl", ZL, lambda i: i ^ 1)


def to_p(value, r):
    return shift(value, "zl", ZL, lambda i: ((i // 2 - r) % 3) * 2 + i % 2)


def to_v(value):
    return shift(value, "y", Y, lambda i: i ^ 1)


def to_u(value, r):
    return shift(value, "y", Y, lambda i: ((i // 2 - r) % 4) * 2 + i % 2)


def to_core(value):
    return shift(value, "core", CORE, lambda i: i ^ 1)


def to_zh(value):
    return shift(value, "zh", ZH, lambda i: i ^ 1)


def product_kernel(near, weight, *refs):
    outs, held, sems = refs[:8], refs[8], refs[9]
    copies = [
        pltpu.make_async_copy(
            weight.at[:, c * 1024 : (c + 1) * 1024], held.at[:, c * 1024 : (c + 1) * 1024], sems.at[c]
        )
        for c in range(8)
    ]
    for copy in copies:
        copy.start()
    for c in range(8):
        copies[c].wait()
        at = slice(c * 1024, (c + 1) * 1024)
        total = jnp.dot(near[...], held[:, at], preferred_element_type=F32)
        for r in range(8):
            outs[r][:, at] = total[r * 24 : (r + 1) * 24].astype(BF)


def products(near, weight):
    whole = pl.BlockSpec(memory_space=pltpu.VMEM)
    return pl.pallas_call(
        product_kernel,
        out_shape=(jax.ShapeDtypeStruct((24, D), BF),) * 8,
        in_specs=[whole, pl.BlockSpec(memory_space=pltpu.HBM)],
        out_specs=(whole,) * 8,
        scratch_shapes=[pltpu.VMEM((256, D), BF), pltpu.SemaphoreType.DMA((8,))],
        compiler_params=pltpu.CompilerParams(vmem_limit_bytes=VMEM),
        cost_estimate=pl.CostEstimate(
            flops=2 * 192 * 256 * D, bytes_accessed=(256 + 192) * 2 * D, transcendentals=0
        ),
        name="products",
    )(near, weight)


def forward_kernel(value, arrived, held, near, out, held_out, near_out):
    out[...] = (value[...].astype(F32) + arrived[...].astype(F32)).astype(BF)
    held_out[...] = held[...]
    near_out[...] = near[...]


def forward(value, arrived, held, near):
    block = pl.BlockSpec((24, 4096), lambda c: (0, c))
    rows = pl.BlockSpec((192, 128), lambda c: (0, c))
    return pl.pallas_call(
        forward_kernel,
        out_shape=(jax.ShapeDtypeStruct((24, D), BF),) * 2 + (jax.ShapeDtypeStruct((192, 256), BF),),
        grid=(2,),
        in_specs=[block] * 3 + [rows],
        out_specs=(block, block, rows),
        compiler_params=pltpu.CompilerParams(vmem_limit_bytes=16 * 1024 * 1024),
        cost_estimate=pl.CostEstimate(flops=24 * D, bytes_accessed=24 * D * 10, transcendentals=0),
        name="forward",
    )(value, arrived, held, near)


def after_q_kernel(keep, left, right, pair, own, one, two):
    total = keep[...].astype(F32) + left[...].astype(F32)
    total = total + right[...].astype(F32) + pair[...].astype(F32)
    own[...] = total[:8]
    one[...] = total[8:16].astype(BF)
    two[...] = total[16:].astype(BF)


def after_q(keep, left, right, pair):
    block = pl.BlockSpec((24, 2048), lambda c: (0, c))
    rows = pl.BlockSpec((8, 2048), lambda c: (0, c))
    return pl.pallas_call(
        after_q_kernel,
        out_shape=tuple(jax.ShapeDtypeStruct((8, D), kind) for kind in (F32, BF, BF)),
        grid=(D // 2048,),
        in_specs=[block] * 4,
        out_specs=(rows,) * 3,
        compiler_params=pltpu.CompilerParams(vmem_limit_bytes=16 * 1024 * 1024),
        cost_estimate=pl.CostEstimate(flops=24 * D * 4, bytes_accessed=24 * D * 10, transcendentals=0),
        name="after_q",
    )(keep, left, right, pair)


def norm_kernel(place, first, second, third, *refs):
    residual, gain, grad_normed, grad_residual, late, normed, grad_mixed, mine, other = refs
    share = first[...] + second[...].astype(F32) + third[...].astype(F32)
    mixed = residual[...].astype(F32) + share
    rms = jnp.sqrt(jnp.mean(mixed * mixed, axis=-1, keepdims=True) + 1e-05)
    unit = mixed / rms
    normed[...] = (unit * gain[...]).astype(BF)
    scaled = grad_normed[...].astype(F32) * gain[...]
    inner = jnp.mean(scaled * unit, axis=-1, keepdims=True)
    grad_mixed[...] = (grad_residual[...].astype(F32) + (scaled - unit * inner) / rms).astype(BF)
    core, zh, v = place[0], place[1], place[2]
    for side in range(2):
        for k in range(2):
            for u in range(4):
                half = (1 - zh) if k == 0 else zh
                at = (half * Y + u * 2 + (v if side == 0 else 1 - v)) * 2
                put = pl.ds(side * 2048 + k * 1024 + u * 256, 256)
                mine[:, put] = grad_mixed[:, pl.ds(pl.multiple_of((at + core) * 256, 256), 256)]
                other[:, put] = grad_mixed[:, pl.ds(pl.multiple_of((at + 1 - core) * 256, 256), 256)]


def norm(place, sums, residual, gain, grad_normed, grad_residual, late):
    whole = pl.BlockSpec(memory_space=pltpu.VMEM)
    count = len(sums) + 4
    return pl.pallas_call(
        norm_kernel,
        out_shape=(
            jax.ShapeDtypeStruct((8, D), BF),
            jax.ShapeDtypeStruct((8, D), BF),
            jax.ShapeDtypeStruct((8, D // 2), BF),
            jax.ShapeDtypeStruct((8, D // 2), BF),
        ),
        in_specs=[pl.BlockSpec(memory_space=pltpu.SMEM)]
        + [whole] * count
        + [pl.BlockSpec(memory_space=pl.ANY)],
        out_specs=(whole,) * 4,
        compiler_params=pltpu.CompilerParams(vmem_limit_bytes=16 * 1024 * 1024),
        cost_estimate=pl.CostEstimate(flops=8 * D * 20, bytes_accessed=8 * D * 20, transcendentals=0),
        name="norm",
    )(place, *sums, residual, gain, grad_normed, grad_residual, late)


def term_kernel(blocks, turned, *refs):
    pieces, outs = refs[:PIECES], refs[PIECES + 1 :]
    for k in range(2):
        for r in range(4):
            at = pl.ds(pl.multiple_of((k * 4 + blocks[r]) * 256, 256), 256)
            block = jnp.concatenate([piece[:, at] for piece in pieces], axis=0)
            total = jnp.dot(turned[...], block, preferred_element_type=F32)
            outs[k * 4 + r][...] = total.astype(outs[k * 4 + r].dtype)


def term_parts(blocks, turned, pieces, late):
    whole = pl.BlockSpec(memory_space=pltpu.VMEM)
    return pl.pallas_call(
        term_kernel,
        out_shape=tuple(jax.ShapeDtypeStruct((256, 256), kind) for kind in (F32, BF, BF, BF) * 2),
        grid=(1,),
        in_specs=[pl.BlockSpec(memory_space=pltpu.SMEM)]
        + [whole] * (1 + PIECES)
        + [pl.BlockSpec(memory_space=pl.ANY)],
        out_specs=(pl.BlockSpec((256, 256), lambda i: (0, 0)),) * 8,
        compiler_params=pltpu.CompilerParams(vmem_limit_bytes=VMEM),
        cost_estimate=pl.CostEstimate(
            flops=2 * 256 * 768 * 2048, bytes_accessed=5 * 1024 * 1024, transcendentals=0
        ),
        name="term",
    )(blocks, turned, *pieces, late)


def back_kernel(count, first, *refs):
    pieces, weight = refs[:count], refs[count]
    out, held, sems = refs[-3:]
    copies = []
    for c in range(8):
        at = pl.ds(pl.multiple_of((first[c // 4] + 4 * (c % 4)) * 256, 256), 256)
        copies.append(pltpu.make_async_copy(weight.at[:, at], held.at[c], sems.at[c]))
        copies[c].start()
    total = jnp.zeros(out.shape, F32)
    for c in range(8):
        copies[c].wait()
        block = jnp.concatenate([piece[:, c * 256 : (c + 1) * 256] for piece in pieces], axis=0)
        total += lax.dot_general(
            block, held[c], (((1,), (1,)), ((), ())), preferred_element_type=F32
        )
    out[...] = total


def back(first, pieces, weight, late):
    whole = pl.BlockSpec(memory_space=pltpu.VMEM)
    rows = sum(piece.shape[0] for piece in pieces)
    return pl.pallas_call(
        functools.partial(back_kernel, len(pieces)),
        out_shape=jax.ShapeDtypeStruct((rows, 256), F32),
        in_specs=[pl.BlockSpec(memory_space=pltpu.SMEM)]
        + [whole] * len(pieces)
        + [pl.BlockSpec(memory_space=pltpu.HBM), pl.BlockSpec(memory_space=pl.ANY)],
        out_specs=whole,
        scratch_shapes=[pltpu.VMEM((8, 256, 256), BF), pltpu.SemaphoreType.DMA((8,))],
        compiler_params=pltpu.CompilerParams(vmem_limit_bytes=VMEM),
        cost_estimate=pl.CostEstimate(
            flops=2 * 256 * rows * 2048, bytes_accessed=3 * 1024 * 1024, transcendentals=0
        ),
        name="back",
    )(first, *pieces, weight, late)


def apart_kernel(*refs):
    pieces, stay, go = refs[:-2], refs[-2], refs[-1]
    place = 0
    for piece in pieces:
        for r in range(piece.shape[0] // 32):
            for k in range(4):
                put = (k // 2) * 192 + place * 8
                out = (stay, go)[k % 2]
                out[put : put + 8, :] = piece[r * 32 + k * 8 : r * 32 + k * 8 + 8, :]
            place += 1


def apart(pieces):
    whole = pl.BlockSpec(memory_space=pltpu.VMEM)
    return pl.pallas_call(
        apart_kernel,
        out_shape=(jax.ShapeDtypeStruct((384, 256), F32),) * 2,
        in_specs=[whole] * len(pieces),
        out_specs=(whole,) * 2,
        compiler_params=pltpu.CompilerParams(vmem_limit_bytes=VMEM),
        cost_estimate=pl.CostEstimate(flops=0, bytes_accessed=1536 * 1024, transcendentals=0),
        name="apart",
    )(*pieces)


def tie_kernel(value, late, out):
    out[...] = value[...]


def tie(value, late):
    whole = pl.BlockSpec(memory_space=pltpu.VMEM)
    return pl.pallas_call(
        tie_kernel,
        out_shape=jax.ShapeDtypeStruct(value.shape, value.dtype),
        in_specs=[whole] * 2,
        out_specs=whole,
        compiler_params=pltpu.CompilerParams(vmem_limit_bytes=VMEM),
        cost_estimate=pl.CostEstimate(flops=0, bytes_accessed=768 * 1024, transcendentals=0),
        name="tie",
    )(value, late)


def per_device(attention, out_proj, residual, gain, grad_normed, grad_residual):
    x, zl, y = lax.axis_index("x"), lax.axis_index("zl"), lax.axis_index("y")
    core, zh = lax.axis_index("core"), lax.axis_index("zh")

    r = jnp.arange(24, dtype=jnp.int32)
    owner_x = (x - r // 6 + X) % X
    owner_q = (zl % 2) ^ ((r // 3) % 2)
    owner_p = (zl // 2 - r % 3 + 3) % 3
    owner = (owner_p * 2 + owner_q) * X + owner_x
    token = jnp.repeat(owner * 8, 8) + jnp.tile(jnp.arange(8, dtype=jnp.int32), 24)
    order = (token[:, None] == jnp.arange(192, dtype=jnp.int32)[None, :]).astype(BF)
    near = jnp.dot(order, attention, preferred_element_type=F32).astype(BF)

    keep, send, one_keep, one_send, left, right, three_keep, three_send = products(near, out_proj)
    left, right = to_x(left, 1), to_x(right, 3)
    right = to_x((three_send.astype(F32) + right.astype(F32)).astype(BF), 3)
    from_right = to_x(one_send, 1)
    left, three_keep, near_late = forward(one_keep, left, three_keep, near)
    left, from_left = to_x(left, 1), to_x(three_keep, 3)
    send = send.astype(F32) + from_right.astype(F32) + right.astype(F32)
    pair = to_q(send.astype(BF))

    far = to_core(near_late)
    both = jnp.concatenate([near.reshape(24, 8, 256), far.reshape(24, 8, 256)], axis=1)
    both = jnp.concatenate([both, to_v(both)], axis=1)
    turned = both.reshape(768, 256).T
    mine, one, two = after_q(keep, left, from_left, pair)
    sums = (mine, to_p(one, 1), to_p(two, 2))

    u, v = y // 2, y % 2
    place = jnp.stack([core, zh, v]).astype(jnp.int32)
    normed, grad_mixed, mine, other = norm(
        place, sums, residual, gain.reshape(1, D), grad_normed, grad_residual, turned
    )
    other = to_core(other)
    blocks = (u - jnp.arange(4, dtype=jnp.int32) + 4) % 4

    own = jnp.concatenate([mine, other], axis=0)
    own = jnp.concatenate([own[:, :2048], to_v(own[:, 2048:])], axis=0)
    line = jnp.concatenate([own, to_p(own, -1), to_p(own, -2)], axis=0)
    lines = (line, to_q(line))
    ones = [to_x(part, -1) for part in lines]
    threes = [to_x(part, -3) for part in lines]
    ones[0] = tie(ones[0], threes[0])
    twos = (to_x(ones[0], -1), to_x(threes[1], -3))
    pieces = [*lines, *ones, *twos, *threes]

    first = jnp.stack([1 - zh, zh]).astype(jnp.int32) * 16 + (v * 2 + core).astype(jnp.int32)
    early = back(first, [*lines, *ones, twos[0], *threes], out_proj, blocks)
    parts = term_parts(blocks, turned, pieces, early)
    got = [[to_u(parts[k * 4 + r], r) for r in (1, 2, 3)] for k in range(2)]
    sums = [parts[k * 4] + sum(value.astype(F32) for value in got[k]) for k in range(2)]
    passing = sums[0].astype(BF)
    grad_out_proj = sums[1] + to_zh(passing).astype(F32)

    late = back(first, twos[1:], out_proj, parts[4])
    stay, go = apart([early[:480], late, early[480:]])
    stay = stay + to_core(go)
    ours = stay[:192] + to_v(stay[192:])
    grad_attention = lax.dot_general(
        order, ours.astype(BF), (((0,), (0,)), ((), ())), preferred_element_type=F32
    ).astype(BF)
    return (normed, grad_mixed, grad_attention, grad_out_proj)


def solution(mesh):
    dp, tensor = ("zh", "y", "core"), ("zl", "x")
    fine = Mesh(mesh.devices.reshape(ZH, Y, CORE, ZL, X), dp + tensor)
    rows = P(dp + tensor, None)
    return jax.shard_map(
        per_device,
        mesh=fine,
        in_specs=(P(dp, tensor), P(tensor, None), rows, P(), rows, rows),
        out_specs=(rows, rows, P(dp, tensor), P(tensor, dp)),
        check_vma=False,
    )
```

```python
import functools

import jax
import jax.numpy as jnp
from jax import lax
from jax.experimental import pallas as pl
from jax.experimental.pallas import tpu as pltpu
from jax.sharding import Mesh, PartitionSpec as P

ZH, Y, CORE, ZL, X = 2, 8, 2, 6, 4
BF, F32 = jnp.bfloat16, jnp.float32
D = 8192
PIECES = 8
VMEM = 24 * 1024 * 1024


def shift(value, axis, size, move):
    return lax.ppermute(value, axis, [(i, move(i)) for i in range(size)])


def to_x(value, r):
    return shift(value, "x", X, lambda i: (i - r) % X)


def to_q(value):
    return shift(value, "zl", ZL, lambda i: i ^ 1)


def to_p(value, r):
    return shift(value, "zl", ZL, lambda i: ((i // 2 - r) % 3) * 2 + i % 2)


def to_v(value):
    return shift(value, "y", Y, lambda i: i ^ 1)


def to_u(value, r):
    return shift(value, "y", Y, lambda i: ((i // 2 - r) % 4) * 2 + i % 2)


def to_core(value):
    return shift(value, "core", CORE, lambda i: i ^ 1)


def to_zh(value):
    return shift(value, "zh", ZH, lambda i: i ^ 1)


def product_kernel(near, weight, *outs):
    for c in range(8):
        at = slice(c * 1024, (c + 1) * 1024)
        total = jnp.dot(near[...], weight[:, at], preferred_element_type=F32)
        for r in range(8):
            outs[r][:, at] = total[r * 24 : (r + 1) * 24].astype(BF)


def products(near, weight):
    whole = pl.BlockSpec(memory_space=pltpu.VMEM)
    return pl.pallas_call(
        product_kernel,
        out_shape=(jax.ShapeDtypeStruct((24, D), BF),) * 8,
        in_specs=[whole] * 2,
        out_specs=(whole,) * 8,
        compiler_params=pltpu.CompilerParams(vmem_limit_bytes=VMEM),
        cost_estimate=pl.CostEstimate(
            flops=2 * 192 * 256 * D, bytes_accessed=(256 + 192) * 2 * D, transcendentals=0
        ),
        name="products",
    )(near, weight)


def forward_kernel(value, arrived, held, near, out, held_out, near_out):
    out[...] = (value[...].astype(F32) + arrived[...].astype(F32)).astype(BF)
    held_out[...] = held[...]
    near_out[...] = near[...]


def forward(value, arrived, held, near):
    block = pl.BlockSpec((24, 4096), lambda c: (0, c))
    rows = pl.BlockSpec((192, 128), lambda c: (0, c))
    return pl.pallas_call(
        forward_kernel,
        out_shape=(jax.ShapeDtypeStruct((24, D), BF),) * 2 + (jax.ShapeDtypeStruct((192, 256), BF),),
        grid=(2,),
        in_specs=[block] * 3 + [rows],
        out_specs=(block, block, rows),
        compiler_params=pltpu.CompilerParams(vmem_limit_bytes=16 * 1024 * 1024),
        cost_estimate=pl.CostEstimate(flops=24 * D, bytes_accessed=24 * D * 10, transcendentals=0),
        name="forward",
    )(value, arrived, held, near)


def after_q_kernel(keep, left, right, pair, own, one, two):
    total = keep[...].astype(F32) + left[...].astype(F32)
    total = total + right[...].astype(F32) + pair[...].astype(F32)
    own[...] = total[:8]
    one[...] = total[8:16].astype(BF)
    two[...] = total[16:].astype(BF)


def after_q(keep, left, right, pair):
    block = pl.BlockSpec((24, 2048), lambda c: (0, c))
    rows = pl.BlockSpec((8, 2048), lambda c: (0, c))
    return pl.pallas_call(
        after_q_kernel,
        out_shape=tuple(jax.ShapeDtypeStruct((8, D), kind) for kind in (F32, BF, BF)),
        grid=(D // 2048,),
        in_specs=[block] * 4,
        out_specs=(rows,) * 3,
        compiler_params=pltpu.CompilerParams(vmem_limit_bytes=16 * 1024 * 1024),
        cost_estimate=pl.CostEstimate(flops=24 * D * 4, bytes_accessed=24 * D * 10, transcendentals=0),
        name="after_q",
    )(keep, left, right, pair)


def norm_kernel(place, first, second, third, *refs):
    residual, gain, grad_normed, grad_residual, late, normed, grad_mixed, mine, other = refs
    share = first[...] + second[...].astype(F32) + third[...].astype(F32)
    mixed = residual[...].astype(F32) + share
    rms = jnp.sqrt(jnp.mean(mixed * mixed, axis=-1, keepdims=True) + 1e-05)
    unit = mixed / rms
    normed[...] = (unit * gain[...]).astype(BF)
    scaled = grad_normed[...].astype(F32) * gain[...]
    inner = jnp.mean(scaled * unit, axis=-1, keepdims=True)
    grad_mixed[...] = (grad_residual[...].astype(F32) + (scaled - unit * inner) / rms).astype(BF)
    core, zh, v = place[0], place[1], place[2]
    for side in range(2):
        for k in range(2):
            for u in range(4):
                half = (1 - zh) if k == 0 else zh
                at = (half * Y + u * 2 + (v if side == 0 else 1 - v)) * 2
                put = pl.ds(side * 2048 + k * 1024 + u * 256, 256)
                mine[:, put] = grad_mixed[:, pl.ds(pl.multiple_of((at + core) * 256, 256), 256)]
                other[:, put] = grad_mixed[:, pl.ds(pl.multiple_of((at + 1 - core) * 256, 256), 256)]


def norm(place, sums, residual, gain, grad_normed, grad_residual, late):
    whole = pl.BlockSpec(memory_space=pltpu.VMEM)
    count = len(sums) + 4
    return pl.pallas_call(
        norm_kernel,
        out_shape=(
            jax.ShapeDtypeStruct((8, D), BF),
            jax.ShapeDtypeStruct((8, D), BF),
            jax.ShapeDtypeStruct((8, D // 2), BF),
            jax.ShapeDtypeStruct((8, D // 2), BF),
        ),
        in_specs=[pl.BlockSpec(memory_space=pltpu.SMEM)]
        + [whole] * count
        + [pl.BlockSpec(memory_space=pl.ANY)],
        out_specs=(whole,) * 4,
        compiler_params=pltpu.CompilerParams(vmem_limit_bytes=16 * 1024 * 1024),
        cost_estimate=pl.CostEstimate(flops=8 * D * 20, bytes_accessed=8 * D * 20, transcendentals=0),
        name="norm",
    )(place, *sums, residual, gain, grad_normed, grad_residual, late)


def term_kernel(blocks, turned, *refs):
    pieces, outs = refs[:PIECES], refs[PIECES + 1 :]
    for k in range(2):
        for r in range(4):
            at = pl.ds(pl.multiple_of((k * 4 + blocks[r]) * 256, 256), 256)
            block = jnp.concatenate([piece[:, at] for piece in pieces], axis=0)
            total = jnp.dot(turned[...], block, preferred_element_type=F32)
            outs[k * 4 + r][...] = total.astype(outs[k * 4 + r].dtype)


def term_parts(blocks, turned, pieces, late):
    whole = pl.BlockSpec(memory_space=pltpu.VMEM)
    return pl.pallas_call(
        term_kernel,
        out_shape=tuple(jax.ShapeDtypeStruct((256, 256), kind) for kind in (F32, BF, BF, BF) * 2),
        grid=(1,),
        in_specs=[pl.BlockSpec(memory_space=pltpu.SMEM)]
        + [whole] * (1 + PIECES)
        + [pl.BlockSpec(memory_space=pl.ANY)],
        out_specs=(pl.BlockSpec((256, 256), lambda i: (0, 0)),) * 8,
        compiler_params=pltpu.CompilerParams(vmem_limit_bytes=VMEM),
        cost_estimate=pl.CostEstimate(
            flops=2 * 256 * 768 * 2048, bytes_accessed=5 * 1024 * 1024, transcendentals=0
        ),
        name="term",
    )(blocks, turned, *pieces, late)


def back_kernel(count, first, *refs):
    pieces, weight, out = refs[:count], refs[count], refs[-1]
    total = jnp.zeros(out.shape, F32)
    for c in range(8):
        at = pl.ds(pl.multiple_of((first[c // 4] + 4 * (c % 4)) * 256, 256), 256)
        block = jnp.concatenate([piece[:, c * 256 : (c + 1) * 256] for piece in pieces], axis=0)
        total += lax.dot_general(
            block, weight[:, at], (((1,), (1,)), ((), ())), preferred_element_type=F32
        )
    out[...] = total


def back(first, pieces, weight, late):
    whole = pl.BlockSpec(memory_space=pltpu.VMEM)
    rows = sum(piece.shape[0] for piece in pieces)
    return pl.pallas_call(
        functools.partial(back_kernel, len(pieces)),
        out_shape=jax.ShapeDtypeStruct((rows, 256), F32),
        in_specs=[pl.BlockSpec(memory_space=pltpu.SMEM)]
        + [whole] * (len(pieces) + 1)
        + [pl.BlockSpec(memory_space=pl.ANY)],
        out_specs=whole,
        compiler_params=pltpu.CompilerParams(vmem_limit_bytes=VMEM),
        cost_estimate=pl.CostEstimate(
            flops=2 * 256 * rows * 2048, bytes_accessed=3 * 1024 * 1024, transcendentals=0
        ),
        name="back",
    )(first, *pieces, weight, late)


def apart_kernel(*refs):
    pieces, stay, go = refs[:-2], refs[-2], refs[-1]
    place = 0
    for piece in pieces:
        for r in range(piece.shape[0] // 32):
            for k in range(4):
                put = (k // 2) * 192 + place * 8
                out = (stay, go)[k % 2]
                out[put : put + 8, :] = piece[r * 32 + k * 8 : r * 32 + k * 8 + 8, :]
            place += 1


def apart(pieces):
    whole = pl.BlockSpec(memory_space=pltpu.VMEM)
    return pl.pallas_call(
        apart_kernel,
        out_shape=(jax.ShapeDtypeStruct((384, 256), F32),) * 2,
        in_specs=[whole] * len(pieces),
        out_specs=(whole,) * 2,
        compiler_params=pltpu.CompilerParams(vmem_limit_bytes=VMEM),
        cost_estimate=pl.CostEstimate(flops=0, bytes_accessed=1536 * 1024, transcendentals=0),
        name="apart",
    )(*pieces)


def tie_kernel(value, late, out):
    out[...] = value[...]


def tie(value, late):
    whole = pl.BlockSpec(memory_space=pltpu.VMEM)
    return pl.pallas_call(
        tie_kernel,
        out_shape=jax.ShapeDtypeStruct(value.shape, value.dtype),
        in_specs=[whole] * 2,
        out_specs=whole,
        compiler_params=pltpu.CompilerParams(vmem_limit_bytes=VMEM),
        cost_estimate=pl.CostEstimate(flops=0, bytes_accessed=768 * 1024, transcendentals=0),
        name="tie",
    )(value, late)


def per_device(attention, out_proj, residual, gain, grad_normed, grad_residual):
    x, zl, y = lax.axis_index("x"), lax.axis_index("zl"), lax.axis_index("y")
    core, zh = lax.axis_index("core"), lax.axis_index("zh")

    r = jnp.arange(24, dtype=jnp.int32)
    owner_x = (x - r // 6 + X) % X
    owner_q = (zl % 2) ^ ((r // 3) % 2)
    owner_p = (zl // 2 - r % 3 + 3) % 3
    owner = (owner_p * 2 + owner_q) * X + owner_x
    token = jnp.repeat(owner * 8, 8) + jnp.tile(jnp.arange(8, dtype=jnp.int32), 24)
    order = (token[:, None] == jnp.arange(192, dtype=jnp.int32)[None, :]).astype(BF)
    near = jnp.dot(order, attention, preferred_element_type=F32).astype(BF)

    keep, send, one_keep, one_send, left, right, three_keep, three_send = products(near, out_proj)
    left, right = to_x(left, 1), to_x(right, 3)
    right = to_x((three_send.astype(F32) + right.astype(F32)).astype(BF), 3)
    from_right = to_x(one_send, 1)
    left, three_keep, near_late = forward(one_keep, left, three_keep, near)
    left, from_left = to_x(left, 1), to_x(three_keep, 3)
    send = send.astype(F32) + from_right.astype(F32) + right.astype(F32)
    pair = to_q(send.astype(BF))

    far = to_core(near_late)
    both = jnp.concatenate([near.reshape(24, 8, 256), far.reshape(24, 8, 256)], axis=1)
    both = jnp.concatenate([both, to_v(both)], axis=1)
    turned = both.reshape(768, 256).T
    mine, one, two = after_q(keep, left, from_left, pair)
    sums = (mine, to_p(one, 1), to_p(two, 2))

    u, v = y // 2, y % 2
    place = jnp.stack([core, zh, v]).astype(jnp.int32)
    normed, grad_mixed, mine, other = norm(
        place, sums, residual, gain.reshape(1, D), grad_normed, grad_residual, turned
    )
    other = to_core(other)
    blocks = (u - jnp.arange(4, dtype=jnp.int32) + 4) % 4

    own = jnp.concatenate([mine, other], axis=0)
    own = jnp.concatenate([own[:, :2048], to_v(own[:, 2048:])], axis=0)
    line = jnp.concatenate([own, to_p(own, -1), to_p(own, -2)], axis=0)
    lines = (line, to_q(line))
    ones = [to_x(part, -1) for part in lines]
    threes = [to_x(part, -3) for part in lines]
    ones[0] = tie(ones[0], threes[0])
    twos = (to_x(ones[0], -1), to_x(threes[1], -3))
    pieces = [*lines, *ones, *twos, *threes]

    first = jnp.stack([1 - zh, zh]).astype(jnp.int32) * 16 + (v * 2 + core).astype(jnp.int32)
    early = back(first, [*lines, ones[0], *threes], out_proj, blocks)
    parts = term_parts(blocks, turned, pieces, early)
    got = [[to_u(parts[k * 4 + r], r) for r in (1, 2, 3)] for k in range(2)]
    sums = [parts[k * 4] + sum(value.astype(F32) for value in got[k]) for k in range(2)]
    passing = sums[0].astype(BF)
    grad_out_proj = sums[1] + to_zh(passing).astype(F32)

    late = back(first, [ones[1], *twos], out_proj, parts[4])
    stay, go = apart([early[:288], late, early[288:]])
    stay = stay + to_core(go)
    ours = stay[:192] + to_v(stay[192:])
    grad_attention = lax.dot_general(
        order, ours.astype(BF), (((0,), (0,)), ((), ())), preferred_element_type=F32
    ).astype(BF)
    return (normed, grad_mixed, grad_attention, grad_out_proj)


def solution(mesh):
    dp, tensor = ("zh", "y", "core"), ("zl", "x")
    fine = Mesh(mesh.devices.reshape(ZH, Y, CORE, ZL, X), dp + tensor)
    rows = P(dp + tensor, None)
    return jax.shard_map(
        per_device,
        mesh=fine,
        in_specs=(P(dp, tensor), P(tensor, None), rows, P(), rows, rows),
        out_specs=(rows, rows, P(dp, tensor), P(tensor, dp)),
        check_vma=False,
    )
```

```python
import functools

import jax
import jax.numpy as jnp
from jax import lax
from jax.experimental import pallas as pl
from jax.experimental.pallas import tpu as pltpu
from jax.sharding import Mesh, PartitionSpec as P

ZH, Y, CORE, ZL, X = 2, 8, 2, 6, 4
BF, F32 = jnp.bfloat16, jnp.float32
D = 8192
PIECES = 8
VMEM = 24 * 1024 * 1024


def shift(value, axis, size, move):
    return lax.ppermute(value, axis, [(i, move(i)) for i in range(size)])


def to_x(value, r):
    return shift(value, "x", X, lambda i: (i - r) % X)


def to_q(value):
    return shift(value, "zl", ZL, lambda i: i ^ 1)


def to_p(value, r):
    return shift(value, "zl", ZL, lambda i: ((i // 2 - r) % 3) * 2 + i % 2)


def to_v(value):
    return shift(value, "y", Y, lambda i: i ^ 1)


def to_u(value, r):
    return shift(value, "y", Y, lambda i: ((i // 2 - r) % 4) * 2 + i % 2)


def to_core(value):
    return shift(value, "core", CORE, lambda i: i ^ 1)


def to_zh(value):
    return shift(value, "zh", ZH, lambda i: i ^ 1)


def product_kernel(order, attention, weight, near, *outs):
    near[...] = jnp.dot(order[...], attention[...], preferred_element_type=F32).astype(BF)
    for c in range(8):
        at = slice(c * 1024, (c + 1) * 1024)
        total = jnp.dot(near[...], weight[:, at], preferred_element_type=F32)
        for r in range(8):
            outs[r][:, at] = total[r * 24 : (r + 1) * 24].astype(BF)


def products(order, attention, weight):
    whole = pl.BlockSpec(memory_space=pltpu.VMEM)
    return pl.pallas_call(
        product_kernel,
        out_shape=(jax.ShapeDtypeStruct((192, 256), BF),) + (jax.ShapeDtypeStruct((24, D), BF),) * 8,
        in_specs=[whole] * 3,
        out_specs=(whole,) * 9,
        compiler_params=pltpu.CompilerParams(vmem_limit_bytes=VMEM),
        cost_estimate=pl.CostEstimate(
            flops=2 * 192 * 256 * D, bytes_accessed=(256 + 192) * 2 * D, transcendentals=0
        ),
        name="products",
    )(order, attention, weight)


def forward_kernel(value, arrived, held, near, out, held_out, near_out):
    out[...] = (value[...].astype(F32) + arrived[...].astype(F32)).astype(BF)
    held_out[...] = held[...]
    near_out[...] = near[...]


def forward(value, arrived, held, near):
    block = pl.BlockSpec((24, 4096), lambda c: (0, c))
    rows = pl.BlockSpec((192, 128), lambda c: (0, c))
    return pl.pallas_call(
        forward_kernel,
        out_shape=(jax.ShapeDtypeStruct((24, D), BF),) * 2 + (jax.ShapeDtypeStruct((192, 256), BF),),
        grid=(2,),
        in_specs=[block] * 3 + [rows],
        out_specs=(block, block, rows),
        compiler_params=pltpu.CompilerParams(vmem_limit_bytes=16 * 1024 * 1024),
        cost_estimate=pl.CostEstimate(flops=24 * D, bytes_accessed=24 * D * 10, transcendentals=0),
        name="forward",
    )(value, arrived, held, near)


def after_q_kernel(keep, left, right, pair, own, one, two):
    total = keep[...].astype(F32) + left[...].astype(F32)
    total = total + right[...].astype(F32) + pair[...].astype(F32)
    own[...] = total[:8]
    one[...] = total[8:16].astype(BF)
    two[...] = total[16:].astype(BF)


def after_q(keep, left, right, pair):
    block = pl.BlockSpec((24, 2048), lambda c: (0, c))
    rows = pl.BlockSpec((8, 2048), lambda c: (0, c))
    return pl.pallas_call(
        after_q_kernel,
        out_shape=tuple(jax.ShapeDtypeStruct((8, D), kind) for kind in (F32, BF, BF)),
        grid=(D // 2048,),
        in_specs=[block] * 4,
        out_specs=(rows,) * 3,
        compiler_params=pltpu.CompilerParams(vmem_limit_bytes=16 * 1024 * 1024),
        cost_estimate=pl.CostEstimate(flops=24 * D * 4, bytes_accessed=24 * D * 10, transcendentals=0),
        name="after_q",
    )(keep, left, right, pair)


def norm_kernel(place, first, second, third, *refs):
    residual, gain, grad_normed, grad_residual, late, normed, grad_mixed, mine, other = refs
    share = first[...] + second[...].astype(F32) + third[...].astype(F32)
    mixed = residual[...].astype(F32) + share
    rms = jnp.sqrt(jnp.mean(mixed * mixed, axis=-1, keepdims=True) + 1e-05)
    unit = mixed / rms
    normed[...] = (unit * gain[...]).astype(BF)
    scaled = grad_normed[...].astype(F32) * gain[...]
    inner = jnp.mean(scaled * unit, axis=-1, keepdims=True)
    grad_mixed[...] = (grad_residual[...].astype(F32) + (scaled - unit * inner) / rms).astype(BF)
    core, zh, v = place[0], place[1], place[2]
    for side in range(2):
        for k in range(2):
            for u in range(4):
                half = (1 - zh) if k == 0 else zh
                at = (half * Y + u * 2 + (v if side == 0 else 1 - v)) * 2
                put = pl.ds(side * 2048 + k * 1024 + u * 256, 256)
                mine[:, put] = grad_mixed[:, pl.ds(pl.multiple_of((at + core) * 256, 256), 256)]
                other[:, put] = grad_mixed[:, pl.ds(pl.multiple_of((at + 1 - core) * 256, 256), 256)]


def norm(place, sums, residual, gain, grad_normed, grad_residual, late):
    whole = pl.BlockSpec(memory_space=pltpu.VMEM)
    count = len(sums) + 4
    return pl.pallas_call(
        norm_kernel,
        out_shape=(
            jax.ShapeDtypeStruct((8, D), BF),
            jax.ShapeDtypeStruct((8, D), BF),
            jax.ShapeDtypeStruct((8, D // 2), BF),
            jax.ShapeDtypeStruct((8, D // 2), BF),
        ),
        in_specs=[pl.BlockSpec(memory_space=pltpu.SMEM)]
        + [whole] * count
        + [pl.BlockSpec(memory_space=pl.ANY)],
        out_specs=(whole,) * 4,
        compiler_params=pltpu.CompilerParams(vmem_limit_bytes=16 * 1024 * 1024),
        cost_estimate=pl.CostEstimate(flops=8 * D * 20, bytes_accessed=8 * D * 20, transcendentals=0),
        name="norm",
    )(place, *sums, residual, gain, grad_normed, grad_residual, late)


def term_kernel(blocks, turned, *refs):
    pieces, outs = refs[:PIECES], refs[PIECES + 1 :]
    for k in range(2):
        for r in range(4):
            at = pl.ds(pl.multiple_of((k * 4 + blocks[r]) * 256, 256), 256)
            block = jnp.concatenate([piece[:, at] for piece in pieces], axis=0)
            total = jnp.dot(turned[...], block, preferred_element_type=F32)
            outs[k * 4 + r][...] = total.astype(outs[k * 4 + r].dtype)


def term_parts(blocks, turned, pieces, late):
    whole = pl.BlockSpec(memory_space=pltpu.VMEM)
    return pl.pallas_call(
        term_kernel,
        out_shape=tuple(jax.ShapeDtypeStruct((256, 256), kind) for kind in (F32, BF, BF, BF) * 2),
        grid=(1,),
        in_specs=[pl.BlockSpec(memory_space=pltpu.SMEM)]
        + [whole] * (1 + PIECES)
        + [pl.BlockSpec(memory_space=pl.ANY)],
        out_specs=(pl.BlockSpec((256, 256), lambda i: (0, 0)),) * 8,
        compiler_params=pltpu.CompilerParams(vmem_limit_bytes=VMEM),
        cost_estimate=pl.CostEstimate(
            flops=2 * 256 * 768 * 2048, bytes_accessed=5 * 1024 * 1024, transcendentals=0
        ),
        name="term",
    )(blocks, turned, *pieces, late)


def back_kernel(count, first, *refs):
    pieces, weight, out = refs[:count], refs[count], refs[-1]
    total = jnp.zeros(out.shape, F32)
    for c in range(8):
        at = pl.ds(pl.multiple_of((first[c // 4] + 4 * (c % 4)) * 256, 256), 256)
        block = jnp.concatenate([piece[:, c * 256 : (c + 1) * 256] for piece in pieces], axis=0)
        total += lax.dot_general(
            block, weight[:, at], (((1,), (1,)), ((), ())), preferred_element_type=F32
        )
    out[...] = total


def back(first, pieces, weight, late):
    whole = pl.BlockSpec(memory_space=pltpu.VMEM)
    rows = sum(piece.shape[0] for piece in pieces)
    return pl.pallas_call(
        functools.partial(back_kernel, len(pieces)),
        out_shape=jax.ShapeDtypeStruct((rows, 256), F32),
        in_specs=[pl.BlockSpec(memory_space=pltpu.SMEM)]
        + [whole] * (len(pieces) + 1)
        + [pl.BlockSpec(memory_space=pl.ANY)],
        out_specs=whole,
        compiler_params=pltpu.CompilerParams(vmem_limit_bytes=VMEM),
        cost_estimate=pl.CostEstimate(
            flops=2 * 256 * rows * 2048, bytes_accessed=3 * 1024 * 1024, transcendentals=0
        ),
        name="back",
    )(first, *pieces, weight, late)


def apart_kernel(*refs):
    pieces, stay, go = refs[:-2], refs[-2], refs[-1]
    place = 0
    for piece in pieces:
        for r in range(piece.shape[0] // 32):
            for k in range(4):
                put = (k // 2) * 192 + place * 8
                out = (stay, go)[k % 2]
                out[put : put + 8, :] = piece[r * 32 + k * 8 : r * 32 + k * 8 + 8, :]
            place += 1


def apart(pieces):
    whole = pl.BlockSpec(memory_space=pltpu.VMEM)
    return pl.pallas_call(
        apart_kernel,
        out_shape=(jax.ShapeDtypeStruct((384, 256), F32),) * 2,
        in_specs=[whole] * len(pieces),
        out_specs=(whole,) * 2,
        compiler_params=pltpu.CompilerParams(vmem_limit_bytes=VMEM),
        cost_estimate=pl.CostEstimate(flops=0, bytes_accessed=1536 * 1024, transcendentals=0),
        name="apart",
    )(*pieces)


def tie_kernel(value, late, out):
    out[...] = value[...]


def tie(value, late):
    whole = pl.BlockSpec(memory_space=pltpu.VMEM)
    return pl.pallas_call(
        tie_kernel,
        out_shape=jax.ShapeDtypeStruct(value.shape, value.dtype),
        in_specs=[whole] * 2,
        out_specs=whole,
        compiler_params=pltpu.CompilerParams(vmem_limit_bytes=VMEM),
        cost_estimate=pl.CostEstimate(flops=0, bytes_accessed=768 * 1024, transcendentals=0),
        name="tie",
    )(value, late)


def per_device(attention, out_proj, residual, gain, grad_normed, grad_residual):
    x, zl, y = lax.axis_index("x"), lax.axis_index("zl"), lax.axis_index("y")
    core, zh = lax.axis_index("core"), lax.axis_index("zh")

    r = jnp.arange(24, dtype=jnp.int32)
    owner_x = (x - r // 6 + X) % X
    owner_q = (zl % 2) ^ ((r // 3) % 2)
    owner_p = (zl // 2 - r % 3 + 3) % 3
    owner = (owner_p * 2 + owner_q) * X + owner_x
    token = jnp.repeat(owner * 8, 8) + jnp.tile(jnp.arange(8, dtype=jnp.int32), 24)
    order = (token[:, None] == jnp.arange(192, dtype=jnp.int32)[None, :]).astype(BF)

    near, keep, send, one_keep, one_send, left, right, three_keep, three_send = products(
        order, attention, out_proj
    )
    left, right = to_x(left, 1), to_x(right, 3)
    right = to_x((three_send.astype(F32) + right.astype(F32)).astype(BF), 3)
    from_right = to_x(one_send, 1)
    left, three_keep, near_late = forward(one_keep, left, three_keep, near)
    left, from_left = to_x(left, 1), to_x(three_keep, 3)
    send = send.astype(F32) + from_right.astype(F32) + right.astype(F32)
    pair = to_q(send.astype(BF))

    far = to_core(near_late)
    both = jnp.concatenate([near.reshape(24, 8, 256), far.reshape(24, 8, 256)], axis=1)
    both = jnp.concatenate([both, to_v(both)], axis=1)
    turned = both.reshape(768, 256).T
    mine, one, two = after_q(keep, left, from_left, pair)
    sums = (mine, to_p(one, 1), to_p(two, 2))

    u, v = y // 2, y % 2
    place = jnp.stack([core, zh, v]).astype(jnp.int32)
    normed, grad_mixed, mine, other = norm(
        place, sums, residual, gain.reshape(1, D), grad_normed, grad_residual, turned
    )
    other = to_core(other)
    blocks = (u - jnp.arange(4, dtype=jnp.int32) + 4) % 4

    own = jnp.concatenate([mine, other], axis=0)
    own = jnp.concatenate([own[:, :2048], to_v(own[:, 2048:])], axis=0)
    line = jnp.concatenate([own, to_p(own, -1), to_p(own, -2)], axis=0)
    lines = (line, to_q(line))
    ones = [to_x(part, -1) for part in lines]
    threes = [to_x(part, -3) for part in lines]
    ones[0] = tie(ones[0], threes[0])
    twos = (to_x(ones[0], -1), to_x(threes[1], -3))
    pieces = [*lines, *ones, *twos, *threes]

    first = jnp.stack([1 - zh, zh]).astype(jnp.int32) * 16 + (v * 2 + core).astype(jnp.int32)
    early = back(first, [*lines, ones[0], *threes], out_proj, blocks)
    parts = term_parts(blocks, turned, pieces, early)
    got = [[to_u(parts[k * 4 + r], r) for r in (1, 2, 3)] for k in range(2)]
    sums = [parts[k * 4] + sum(value.astype(F32) for value in got[k]) for k in range(2)]
    passing = sums[0].astype(BF)
    grad_out_proj = sums[1] + to_zh(passing).astype(F32)

    late = back(first, [ones[1], *twos], out_proj, parts[4])
    stay, go = apart([early[:288], late, early[288:]])
    stay = stay + to_core(go)
    ours = stay[:192] + to_v(stay[192:])
    grad_attention = lax.dot_general(
        order, ours.astype(BF), (((0,), (0,)), ((), ())), preferred_element_type=F32
    ).astype(BF)
    return (normed, grad_mixed, grad_attention, grad_out_proj)


def solution(mesh):
    dp, tensor = ("zh", "y", "core"), ("zl", "x")
    fine = Mesh(mesh.devices.reshape(ZH, Y, CORE, ZL, X), dp + tensor)
    rows = P(dp + tensor, None)
    return jax.shard_map(
        per_device,
        mesh=fine,
        in_specs=(P(dp, tensor), P(tensor, None), rows, P(), rows, rows),
        out_specs=(rows, rows, P(dp, tensor), P(tensor, dp)),
        check_vma=False,
    )
```
